512 devices in a mesh: group: 16 (over y, core), member: 32 (over x, z).
Axes of the slice: x: 4, y: 8, z: 8, core: 2. Of those that a mesh axis runs over, the one named last changes fastest.
Arguments:
- grid_feats: bfloat16 [1048576, 256], P(('group', 'member')), may hold values from -6 to 6
- grid_owner: int32 [1048576, 1], P(('group', 'member')), may hold values from 0 to 31; in each aligned block of 2048 rows (0 to 2047, 2048 to 4095, ...) at most 256 rows name the same one
- grid_slot: int32 [1048576, 1], P(('group', 'member')), may hold values from 0 to 1023
- mesh_states: bfloat16 [524288, 256], P(('group', 'member')), may hold values from -6 to 6
- coarse_states: bfloat16 [65536, 256], P(('group', 'member')), may hold values from -6 to 6
- coarse_ids: int32 [524288, 4], P(('group', 'member')), may hold values from 0 to 8191
- tile_cols: int32 [4096, 4], P(('group', 'member')), may hold values from 0 to 23
- adjacency: bfloat16 [4096, 4, 128, 128], P(('group', 'member')), may hold values from -0.26367188 to 0.26367188
- w_encode: bfloat16 [256, 256], replicated, may hold values from -0.375 to 0.375
- w_fine: bfloat16 [256, 256], replicated, may hold values from -0.375 to 0.375
- w_coarse: bfloat16 [256, 256], replicated, may hold values from -0.375 to 0.375
- w_edge: bfloat16 [256, 256], replicated, may hold values from -0.375 to 0.375
- w_sender: bfloat16 [256, 256], replicated, may hold values from -0.375 to 0.375
- w_node_in: bfloat16 [1024, 256], replicated, may hold values from -0.1875 to 0.1875
- w_node_out: bfloat16 [256, 256], replicated, may hold values from -0.375 to 0.375
- node_gain: float32 [256], replicated, may hold values from 0.1 to 1.9
Outputs:
- new_states: bfloat16 [524288, 256], P(('group', 'member'))
The draws below stay inside these ranges and needn't reach their ends.
Inputs may be any that keep to these rules, and one draw needn't show every extreme that they name: `grid_owner`: the rows of one device name each owner at most 256 times, a bound that some block reaches.
All inputs are finite; a program needn't handle non-finite values.
Results may differ from the reference program's by a relative error of at most 0.012.
Values may be sent and summed in bfloat16 or wider, within the bound.
A program may use at most 64 MiB of HBM per device.

```python
import math
import jax
import jax.numpy as jnp
import numpy as np
from jax import lax

D = 256
GR = 2048
MN_DEV = 1024
K = 4
TPR = 4
TILE = 128
CAP = 256
TD = 8
CG = 4096
GRID_ROWS = 1048576
NODES = 524288
COARSE = 65536
N_GROUP = 16
N_MEMBER = 32


def with_ends(array, key, least, largest):
    spot = [jax.random.randint(jax.random.fold_in(key, axis), (), 0, length) for axis, length in enumerate(array.shape)]
    main_axis = array.shape.index(max(array.shape))
    next_to = spot[:main_axis] + [(spot[main_axis] + 1) % array.shape[main_axis]] + spot[main_axis + 1:]
    return array.at[tuple(spot)].set(least).at[tuple(next_to)].set(largest)


def block_levels(rng, dims, split, smallest, high):
    factor_of, own = 1.0, jax.random.fold_in(rng, 6)
    for dim, shards_of in split:
        steps = jnp.exp(jax.random.uniform(jax.random.fold_in(own, dim), (shards_of,), jnp.float32, smallest / len(split), high / len(split)))
        factor_of = factor_of * jnp.repeat(steps, dims[dim] // shards_of).reshape([-1 if axis == dim else 1 for axis in range(len(dims))])
    return factor_of


def assign_block(own_key, own, number, rows, count, top, bound, slope):
    sequence = jax.random.permutation(own_key, count)
    heavy_load, usual = shares(count, rows * top, bound, slope, True), shares(count, rows * top, bound, slope, False)
    places = jnp.arange(count)

    def named(tallies, turn):
        used = int((tallies > 0).sum())
        fixed = max(1, used // 4)
        moved = fixed + (places - fixed + turn * (used - fixed)) % max(1, count - fixed)
        return jnp.zeros((count,), jnp.int32).at[sequence[jnp.where(places < fixed, places, moved)]].set(jnp.asarray(tallies, jnp.int32))

    tallies = jnp.where(number % 4 == 0, named(heavy_load, number // 4), named(usual, number - number // 4 - 1))
    mixed = jax.random.permutation(jax.random.fold_in(own, 3), count)
    source_of, sink = mixed[0:count // 2 * 2:2], mixed[1:count // 2 * 2:2]
    room = jnp.minimum(tallies[source_of] - 1, bound - tallies[sink]) // 2
    room = jnp.where((source_of == sequence[0]) | (sink == sequence[0]) | (tallies[sink] == 0), 0, jnp.maximum(room, 0))
    moved = jax.random.randint(jax.random.fold_in(own, 4), (count // 2,), 0, 1 << 20) % (room + 1)
    tallies = tallies.at[source_of].add(-moved).at[sink].add(moved)
    items = jnp.searchsorted(jnp.cumsum(tallies), jnp.arange(rows * top), side="right").astype(jnp.int32)
    table = items.reshape(top, rows).T
    table = table[jax.random.permutation(jax.random.fold_in(own, 1), rows)]
    turn = jax.random.randint(jax.random.fold_in(own, 2), (rows, 1), 0, top)
    return jnp.take_along_axis(table, (jnp.arange(top)[None, :] + turn) % top, axis=1)


def shares(amount, total, reach, skew, full):
    loads = [(1 << 20) // math.isqrt(standing ** skew) + 1 for standing in range(1, amount + 1)]
    largest = reach if full else min(reach, max(-(-total // amount), total * loads[0] // sum(loads)))
    least = 1 if total - largest >= amount - 1 else 0
    counts, surplus = [largest] + [least] * (amount - 1), total - largest - least * (amount - 1)
    while surplus > 0:
        candidates = [i for i in range(1, amount) if counts[i] < largest] or [i for i in range(1, amount) if counts[i] < reach]
        pool, budget = sum([loads[i] for i in candidates]), surplus
        for i in candidates:
            addition = min(reach - counts[i], max(1, budget * loads[i] // pool), surplus)
            counts[i] = counts[i] + addition
            surplus = surplus - addition
    return np.array(counts)


def bell_draw(rng, shape, spread, most, cuts=(), held_as=jnp.bfloat16):
    values = jax.random.normal(rng, shape, jnp.float32) * spread
    if len(cuts) > 0:
        values = block_levels(rng, shape, cuts, -0.22, 0.18) * values
    return jnp.clip(values, min=-most, max=most).astype(held_as)


def setup_inputs(seed: int = 0) -> dict:
    seeds = jax.random.split(jax.random.key(seed), 17)
    grid_feats = bell_draw(seeds[0], (GRID_ROWS, D), 1.0, 6.0, ((0, 512),))
    grid_owner_keys = jax.random.split(jax.random.fold_in(seeds[1], 1), GRID_ROWS // GR)
    grid_owner_turns = jax.random.permutation(jax.random.fold_in(seeds[1], 3), GRID_ROWS // GR)
    grid_owner = jax.vmap(lambda own, number: assign_block(jax.random.fold_in(seeds[1], 2), own, number, GR, N_MEMBER, 1, CAP, 2))(grid_owner_keys, grid_owner_turns).reshape((GRID_ROWS, 1))
    grid_slot = with_ends(jax.random.randint(seeds[2], (GRID_ROWS, 1), 0, MN_DEV), jax.random.fold_in(seeds[2], 1), 0, MN_DEV - 1).astype(jnp.int32)
    mesh_states = bell_draw(seeds[3], (NODES, D), 1.0, 6.0, ((0, 512),))
    coarse_states = bell_draw(seeds[4], (COARSE, D), 1.0, 6.0, ((0, 512),))
    coarse_ids = with_ends(jax.random.randint(seeds[5], (NODES, K), 0, 2 * CG), jax.random.fold_in(seeds[5], 1), 0, (2 * CG) - 1).astype(jnp.int32)
    tile_cols = with_ends(jax.random.randint(seeds[6], (NODES // TILE, TPR), 0, 3 * TD), jax.random.fold_in(seeds[6], 1), 0, (3 * TD) - 1).astype(jnp.int32)
    adjacency = bell_draw(seeds[7], (NODES // TILE, TPR, TILE, TILE), ((TPR * TILE) ** -0.5), 0.26367188, ((0, 512),))
    w_encode = bell_draw(seeds[8], (D, D), D ** -0.5, 0.375)
    w_fine = bell_draw(seeds[9], (D, D), D ** -0.5, 0.375)
    w_coarse = bell_draw(seeds[10], (D, D), D ** -0.5, 0.375)
    w_edge = bell_draw(seeds[11], (D, D), D ** -0.5, 0.375)
    w_sender = bell_draw(seeds[12], (D, D), D ** -0.5, 0.375)
    w_node_in = bell_draw(seeds[13], (4 * D, D), (4 * D) ** -0.5, 0.1875)
    w_node_out = bell_draw(seeds[14], (D, D), D ** -0.5, 0.375)
    node_gain = jnp.clip(1.0 + 0.18 * jax.random.normal(seeds[15], (D,), jnp.float32), 0.1, 1.9)
    return dict(grid_feats=grid_feats, grid_owner=grid_owner, grid_slot=grid_slot, mesh_states=mesh_states, coarse_states=coarse_states, coarse_ids=coarse_ids, tile_cols=tile_cols, adjacency=adjacency, w_encode=w_encode, w_fine=w_fine, w_coarse=w_coarse, w_edge=w_edge, w_sender=w_sender, w_node_in=w_node_in, w_node_out=w_node_out, node_gain=node_gain)


def reference(grid_feats, grid_owner, grid_slot, mesh_states, coarse_states, coarse_ids, tile_cols, adjacency, w_encode, w_fine, w_coarse, w_edge, w_sender, w_node_in, w_node_out, node_gain):
    tiles_dev = MN_DEV // TILE
    region = N_MEMBER * MN_DEV
    rows_group = N_MEMBER * GR
    projected = jnp.dot(coarse_states, w_coarse, preferred_element_type=jnp.float32).astype(jnp.bfloat16)

    def one_group(group_index):
        g = group_index.astype(jnp.int32)
        grid_g = lax.dynamic_slice_in_dim(grid_feats, (g * rows_group).astype(jnp.int32), rows_group, 0)
        owner_g = lax.dynamic_slice_in_dim(grid_owner, (g * rows_group).astype(jnp.int32), rows_group, 0)[:, 0]
        slot_g = lax.dynamic_slice_in_dim(grid_slot, (g * rows_group).astype(jnp.int32), rows_group, 0)[:, 0]
        messages = jax.nn.silu(jnp.dot(grid_g, w_encode, preferred_element_type=jnp.float32)).astype(jnp.bfloat16)
        target = (owner_g * MN_DEV + slot_g).astype(jnp.int32)
        encoded = jax.ops.segment_sum(messages.astype(jnp.float32), target, num_segments=region).astype(jnp.bfloat16)
        states = lax.dynamic_slice_in_dim(mesh_states, (g * region).astype(jnp.int32), region, 0)
        own_rows = lax.dynamic_slice_in_dim(projected, (g * CG).astype(jnp.int32), CG, 0)
        prior = ((g + N_GROUP - 1) % N_GROUP).astype(jnp.int32)
        prior_rows = lax.dynamic_slice_in_dim(projected, (prior * CG).astype(jnp.int32), CG, 0)
        table = jnp.concatenate([own_rows, prior_rows], axis=0)
        ids = lax.dynamic_slice_in_dim(coarse_ids, (g * region).astype(jnp.int32), region, 0)
        fine_part = jnp.dot(states, w_fine, preferred_element_type=jnp.float32)
        edge_hidden = jax.nn.silu(fine_part[:, None, :] + table[ids].astype(jnp.float32)).astype(jnp.bfloat16)
        coarse_sum = jnp.einsum('nkd,de->ne', edge_hidden.astype(jnp.float32), w_edge.astype(jnp.float32)).astype(jnp.bfloat16)
        sent = jax.nn.silu(jnp.dot(states, w_sender, preferred_element_type=jnp.float32)).astype(jnp.bfloat16)
        blocks = sent.reshape(N_MEMBER, tiles_dev, TILE, D)
        zero_block = jnp.zeros((1, tiles_dev, TILE, D), jnp.bfloat16)
        earlier = jnp.concatenate([zero_block, blocks[:-1]], axis=0)
        later = jnp.concatenate([blocks[1:], zero_block], axis=0)
        window = jnp.concatenate([earlier, blocks, later], axis=1)
        cols = lax.dynamic_slice_in_dim(tile_cols, (g * N_MEMBER * tiles_dev).astype(jnp.int32), N_MEMBER * tiles_dev, 0).reshape(N_MEMBER, tiles_dev, TPR)
        weights = lax.dynamic_slice_in_dim(adjacency, (g * N_MEMBER * tiles_dev).astype(jnp.int32), N_MEMBER * tiles_dev, 0).reshape(N_MEMBER, tiles_dev, TPR, TILE, TILE)

        def one_member(packed):
            member_window, member_cols, member_weights = packed
            chosen = member_window[member_cols]
            return jnp.einsum('rkij,rkjd->rid', member_weights.astype(jnp.float32), chosen.astype(jnp.float32))
        mesh_sum = lax.map(one_member, (window, cols, weights)).reshape(region, D).astype(jnp.bfloat16)
        joined = jnp.concatenate([states, encoded, coarse_sum, mesh_sum], axis=1)
        hidden = jax.nn.silu(jnp.dot(joined, w_node_in, preferred_element_type=jnp.float32)).astype(jnp.bfloat16)
        update = jnp.dot(hidden, w_node_out, preferred_element_type=jnp.float32)
        mean = lax.optimization_barrier(jnp.mean(update, axis=1, keepdims=True))
        centred = update - mean
        variance = lax.optimization_barrier(jnp.mean(centred * centred, axis=1, keepdims=True))
        normed = centred / jnp.sqrt(variance + 1e-05) * node_gain
        return (states.astype(jnp.float32) + normed).astype(jnp.bfloat16)
    result = lax.map(one_group, jnp.arange(N_GROUP, dtype=jnp.int32))
    return result.reshape(NODES, D)
```

```python
import functools

import jax
import jax.numpy as jnp
from jax import lax
from jax.experimental import pallas as pl
from jax.experimental.pallas import tpu as pltpu
from jax.sharding import PartitionSpec as P

MESH = pl.DeviceIdType.MESH
F32 = jnp.float32
BF16 = jnp.bfloat16
LINE = 8
PART = 112
SLOT = 128


def silu(v):
    return v / (1.0 + jnp.exp(-v))


def dot(a, b):
    return jnp.dot(a, b, preferred_element_type=F32)


def dot_t(a, b):
    return lax.dot_general(a, b, (((1,), (1,)), ((), ())), preferred_element_type=F32)


def kernel(
    groups,
    members,
    line,
    ids_ref,
    cols_ref,
    feats_ref,
    owner_ref,
    slot_ref,
    mesh_ref,
    coarse_ref,
    adj_ref,
    w_encode_ref,
    w_fine_ref,
    w_coarse_ref,
    w_edge_ref,
    w_sender_ref,
    w_in_ref,
    w_out_ref,
    gain_ref,
    out_ref,
    messages,
    send1,
    recv1,
    send_idx,
    recv_idx,
    table16,
    table32,
    window,
    picked,
    fine,
    partial,
    total,
    enc_send,
    enc,
    s_a2a,
    r_a2a,
    s_idx,
    r_idx,
    s_enc,
    r_enc,
    s_line,
    r_line,
    s_plane,
    r_plane,
    s_next,
    r_next,
    s_halo,
    r_halo,
):
    me_g = lax.axis_index("group")
    me = lax.axis_index("member")
    lines = members // line
    my_line = me // line
    my_spot = me % line
    rows, width = feats_ref.shape
    nodes = mesh_ref.shape[0]
    own = coarse_ref.shape[0]
    neighbours = ids_ref.shape[0] // nodes
    tile = adj_ref.shape[2]
    tiles = adj_ref.shape[0]
    per_tile = adj_ref.shape[1]
    blk = nodes // members
    next_g = (me_g + 1) % groups
    prev_g = (me_g + groups - 1) % groups

    def copy(src, dst, send, recv, group, member):
        return pltpu.make_async_remote_copy(
            src_ref=src,
            dst_ref=dst,
            send_sem=send,
            recv_sem=recv,
            device_id=(group, member),
            device_id_type=MESH,
        )

    barrier = pltpu.get_barrier_semaphore()

    @pl.loop(1, members)
    def _(d):
        pl.semaphore_signal(
            barrier, inc=1, device_id=(me_g, (me + d) % members), device_id_type=MESH
        )

    pl.semaphore_signal(barrier, inc=1, device_id=(next_g, me), device_id_type=MESH)
    pl.semaphore_signal(barrier, inc=1, device_id=(prev_g, me), device_id_type=MESH)

    table16[0, my_line, pl.ds(pl.multiple_of(my_spot * own, own), own), :] = dot(
        coarse_ref[...], w_coarse_ref[...]
    ).astype(BF16)
    chunk = 256

    @pl.loop(0, nodes // chunk)
    def _(i):
        at = pl.ds(pl.multiple_of(i * chunk, chunk), chunk)
        per = chunk // tile
        part = silu(dot(mesh_ref[at, :], w_sender_ref[...])).astype(BF16)
        window[pl.ds(tiles + i * per, per)] = part.reshape(per, tile, width)

    @pl.when(me == 0)
    def _():
        window[0:tiles] = jnp.zeros((tiles, tile, width), BF16)

    @pl.when(me == members - 1)
    def _():
        window[2 * tiles : 3 * tiles] = jnp.zeros((tiles, tile, width), BF16)

    recv1[:, PART:, :] = jnp.zeros((members, SLOT - PART, width), BF16)

    pl.semaphore_wait(barrier, members + 1)

    def line_copy(spot, at_spot):
        at = pl.ds(pl.multiple_of(at_spot * own, own), own)
        block = table16.at[0, my_line, at, :]
        return copy(
            block, block, s_line.at[spot], r_line.at[at_spot], me_g, my_line * line + spot
        )

    @pl.loop(1, line)
    def _(d):
        line_copy((my_spot + d) % line, my_spot).start()

    def halo_up():
        return copy(
            window.at[tiles : 2 * tiles],
            window.at[0:tiles],
            s_halo.at[0],
            r_halo.at[0],
            me_g,
            (me + 1) % members,
        )

    def halo_down():
        return copy(
            window.at[tiles : 2 * tiles],
            window.at[2 * tiles : 3 * tiles],
            s_halo.at[1],
            r_halo.at[1],
            me_g,
            (me + members - 1) % members,
        )

    @pl.when(me < members - 1)
    def _():
        halo_up().start()

    @pl.when(me > 0)
    def _():
        halo_down().start()

    @pl.loop(0, rows // chunk)
    def _(i):
        at = pl.ds(pl.multiple_of(i * chunk, chunk), chunk)
        messages[at, :] = silu(dot(feats_ref[at, :], w_encode_ref[...])).astype(BF16)

    owner = owner_ref[...]
    slot = slot_ref[...]
    way = (slot // blk + owner) % members
    hot = (lax.broadcasted_iota(jnp.int32, (members, rows), 0) == way).astype(F32)
    hot16 = hot.astype(BF16)
    lanes = min(256, rows)
    upper = (
        lax.broadcasted_iota(jnp.int32, (lanes, lanes), 0)
        < lax.broadcasted_iota(jnp.int32, (lanes, lanes), 1)
    ).astype(BF16)
    before = jnp.zeros((members, 1), F32)
    ranks = []
    for b in range(rows // lanes):
        here = hot[:, b * lanes : (b + 1) * lanes]
        count = dot(hot16[:, b * lanes : (b + 1) * lanes], upper) + before
        ranks.append(jnp.sum(here * count, axis=0, keepdims=True))
        before = before + jnp.sum(here, axis=1, keepdims=True)
    rank = jnp.concatenate(ranks, axis=1).astype(jnp.int32)
    fits = rank < PART
    dest = jnp.where(fits, way * SLOT + rank, -1)
    stack = jnp.concatenate(
        [
            hot16,
            hot16 * owner.astype(F32).astype(BF16),
            hot16 * (slot % blk).astype(F32).astype(BF16),
        ],
        axis=0,
    )
    place = (
        lax.broadcasted_iota(jnp.int32, (SLOT, rows), 0) == jnp.where(fits, rank, -1)
    ).astype(BF16)
    found = dot_t(stack, place)
    index = jnp.where(
        found[:members] > 0.5,
        found[members : 2 * members] * blk + found[2 * members :],
        -1.0,
    ).astype(jnp.int32)
    for t in range(members):
        send_idx[t] = index[t : t + 1, :]

    def row_copy(to, source):
        return copy(
            send1.at[to, 0:PART, :],
            recv1.at[source, 0:PART, :],
            s_a2a.at[to],
            r_a2a.at[source],
            me_g,
            to,
        )

    def idx_copy(to, source):
        return copy(
            send_idx.at[to], recv_idx.at[source], s_idx.at[to], r_idx.at[source], me_g, to
        )

    batch = 4

    @pl.loop(0, members // batch)
    def _(step):
        first = ((me // batch + step) % (members // batch)) * batch
        spread = (
            lax.broadcasted_iota(jnp.int32, (batch * SLOT, rows), 0) + first * SLOT == dest
        ).astype(BF16)
        packed = dot(spread, messages[...]).astype(BF16)
        for j in range(batch):
            to = first + j
            send1[to] = packed[j * SLOT : (j + 1) * SLOT]

            @pl.when(to != me)
            def _():
                row_copy(to, me).start()
                idx_copy(to, me).start()

    recv1[me, 0:PART, :] = send1[me, 0:PART, :]
    recv_idx[me] = send_idx[me]

    @pl.loop(1, line)
    def _(d):
        line_copy(my_spot, (my_spot + d) % line).wait_recv()

    def plane_copy(to_line, at_line):
        block = table16.at[0, at_line]
        return copy(
            block, block, s_plane.at[to_line], r_plane.at[at_line], me_g, to_line * line + my_spot
        )

    def next_copy(at_line):
        return copy(
            table16.at[0, at_line],
            table16.at[1, at_line],
            s_next.at[at_line],
            r_next.at[at_line],
            next_g,
            me,
        )

    @pl.loop(1, lines)
    def _(d):
        plane_copy((my_line + d) % lines, my_line).start()

    next_copy(my_line).start()

    @pl.loop(0, nodes // chunk)
    def _(i):
        at = pl.ds(pl.multiple_of(i * chunk, chunk), chunk)
        fine[at, :] = dot(mesh_ref[at, :], w_fine_ref[...])
        partial[at, :] = dot(mesh_ref[at, :], w_in_ref[0:width, :])

    @pl.when(me > 0)
    def _():
        halo_up().wait_recv()

    @pl.when(me < members - 1)
    def _():
        halo_down().wait_recv()

    @pl.loop(0, tiles)
    def _(r):
        acc = jnp.zeros((tile, width), F32)
        for j in range(per_tile):
            acc = acc + dot(adj_ref[r, j], window[cols_ref[r * per_tile + j]])
        at = pl.ds(pl.multiple_of(r * tile, tile), tile)
        partial[at, :] += dot(acc.astype(BF16), w_in_ref[3 * width : 4 * width, :])

    @pl.loop(1, lines)
    def _(d):
        at_line = (my_line + d) % lines
        plane_copy(my_line, at_line).wait_recv()
        next_copy(at_line).start()

    half = own * members

    def widen(part, at_line):
        at = pl.ds(pl.multiple_of(part * half + at_line * line * own, own), line * own)
        table32[at, :] = table16[part, at_line].astype(F32)

    @pl.loop(0, lines)
    def _(i):
        widen(0, i)

    @pl.loop(0, lines)
    def _(i):
        next_copy(i).wait_recv()
        widen(1, i)

    unroll = 8

    @pl.loop(0, nodes // unroll)
    def _(i):
        for u in range(unroll):
            for k in range(neighbours):
                n = i * unroll + u
                picked[k, pl.ds(n, 1), :] = table32[pl.ds(ids_ref[n * neighbours + k], 1), :]

    @pl.loop(0, nodes // chunk)
    def _(i):
        at = pl.ds(pl.multiple_of(i * chunk, chunk), chunk)
        acc = jnp.zeros((chunk, width), F32)
        for k in range(neighbours):
            acc = acc + silu(fine[at, :] + picked[k, at, :]).astype(BF16).astype(F32)
        coarse_sum = dot(acc.astype(BF16), w_edge_ref[...]).astype(BF16)
        partial[at, :] += dot(coarse_sum, w_in_ref[2 * width : 3 * width, :])

    total[...] = jnp.zeros_like(total)

    @pl.loop(0, members // 2)
    def _(i):
        sources = [(me + members - 2 * i - j) % members for j in range(2)]
        for source in sources:

            @pl.when(source != me)
            def _():
                row_copy(me, source).wait_recv()
                idx_copy(me, source).wait_recv()

        index = jnp.concatenate([recv_idx[source] for source in sources], axis=1)
        block = jnp.concatenate([recv1[source] for source in sources], axis=0)
        spread = (
            lax.broadcasted_iota(jnp.int32, (nodes, 2 * SLOT), 0) == index
        ).astype(BF16)
        total[...] += dot(spread, block)

    enc_send[...] = total[...].astype(BF16)

    def enc_copy(to, source):
        there = (source + members - to) % members
        return copy(
            enc_send.at[pl.ds(pl.multiple_of(to * blk, blk), blk), :],
            enc.at[pl.ds(pl.multiple_of(there * blk, blk), blk), :],
            s_enc.at[to],
            r_enc.at[source],
            me_g,
            to,
        )

    @pl.loop(1, members)
    def _(d):
        enc_copy((me + d) % members, me).start()

    enc[0:blk, :] = enc_send[pl.ds(pl.multiple_of(me * blk, blk), blk), :]

    @pl.loop(1, members)
    def _(d):
        enc_copy(me, (me + d) % members).wait_recv()

    @pl.loop(0, nodes // chunk)
    def _(i):
        at = pl.ds(pl.multiple_of(i * chunk, chunk), chunk)
        hidden = silu(partial[at, :] + dot(enc[at, :], w_in_ref[width : 2 * width, :]))
        update = dot(hidden.astype(BF16), w_out_ref[...])
        mean = jnp.mean(update, axis=1, keepdims=True)
        centred = update - mean
        variance = jnp.mean(centred * centred, axis=1, keepdims=True)
        normed = centred / jnp.sqrt(variance + 1e-05) * gain_ref[...]
        out_ref[at, :] = (mesh_ref[at, :].astype(F32) + normed).astype(BF16)

    @pl.loop(1, line)
    def _(d):
        line_copy((my_spot + d) % line, my_spot).wait_send()

    @pl.loop(1, lines)
    def _(d):
        plane_copy((my_line + d) % lines, my_line).wait_send()

    @pl.loop(0, lines)
    def _(i):
        next_copy(i).wait_send()

    @pl.when(me < members - 1)
    def _():
        halo_up().wait_send()

    @pl.when(me > 0)
    def _():
        halo_down().wait_send()

    @pl.loop(1, members)
    def _(d):
        to = (me + d) % members
        row_copy(to, me).wait_send()
        idx_copy(to, me).wait_send()
        enc_copy(to, me).wait_send()


def fast(
    groups,
    members,
    grid_feats,
    owner,
    slot,
    mesh_states,
    coarse_states,
    coarse_ids,
    tile_cols,
    adjacency,
    w_encode,
    w_fine,
    w_coarse,
    w_edge,
    w_sender,
    w_node_in,
    w_node_out,
    node_gain,
):
    rows, width = grid_feats.shape
    nodes = mesh_states.shape[0]
    own = coarse_states.shape[0]
    neighbours = coarse_ids.shape[1]
    tiles, per_tile, tile, _ = adjacency.shape
    line = min(LINE, members // 2)
    lines = members // line
    dma = pltpu.SemaphoreType.DMA
    vmem = pl.BlockSpec(memory_space=pltpu.VMEM)
    smem = pl.BlockSpec(memory_space=pltpu.SMEM)
    return pl.pallas_call(
        functools.partial(kernel, groups, members, line),
        out_shape=jax.ShapeDtypeStruct((nodes, width), BF16),
        in_specs=[smem] * 2 + [vmem] * 14,
        out_specs=vmem,
        scratch_shapes=[
            pltpu.VMEM((rows, width), BF16),
            pltpu.VMEM((members, SLOT, width), BF16),
            pltpu.VMEM((members, SLOT, width), BF16),
            pltpu.VMEM((members, 1, SLOT), jnp.int32),
            pltpu.VMEM((members, 1, SLOT), jnp.int32),
            pltpu.VMEM((2, lines, line * own, width), BF16),
            pltpu.VMEM((2 * members * own, width), F32),
            pltpu.VMEM((3 * tiles, tile, width), BF16),
            pltpu.VMEM((neighbours, nodes, width), F32),
            pltpu.VMEM((nodes, width), F32),
            pltpu.VMEM((nodes, width), F32),
            pltpu.VMEM((nodes, width), F32),
            pltpu.VMEM((nodes, width), BF16),
            pltpu.VMEM((nodes, width), BF16),
            dma((members,)),
            dma((members,)),
            dma((members,)),
            dma((members,)),
            dma((members,)),
            dma((members,)),
            dma((line,)),
            dma((line,)),
            dma((lines,)),
            dma((lines,)),
            dma((lines,)),
            dma((lines,)),
            dma((2,)),
            dma((2,)),
        ],
        compiler_params=pltpu.CompilerParams(
            collective_id=0, has_side_effects=True, vmem_limit_bytes=56 << 20
        ),
    )(
        coarse_ids.reshape(-1),
        tile_cols.reshape(-1),
        grid_feats,
        owner.reshape(1, rows),
        slot.reshape(1, rows),
        mesh_states,
        coarse_states,
        adjacency,
        w_encode,
        w_fine,
        w_coarse,
        w_edge,
        w_sender,
        w_node_in,
        w_node_out,
        node_gain.reshape(1, width),
    )


def from_behind(block, axis, distance):
    devices = range(lax.axis_size(axis))
    route = [((i - distance) % len(devices), i) for i in devices]
    return lax.ppermute(block, axis, route)


def with_halo(cells, sides, width):
    for axis, dim in sides:
        count = lax.axis_size(axis)
        ends = count - 1
        head = lax.slice_in_dim(cells, 0, width, axis=dim)
        tail = lax.slice_in_dim(cells, cells.shape[dim] - width, cells.shape[dim], axis=dim)
        cells = jnp.concatenate(
            [
                lax.ppermute(tail, axis, [(i, (i + 1) % count) for i in range(ends)]),
                cells,
                lax.ppermute(head, axis, [((i + 1) % count, i) for i in range(ends)]),
            ],
            axis=dim,
        )
    return cells


def slow(
    grid_feats,
    grid_owner,
    grid_slot,
    mesh_states,
    coarse_states,
    coarse_ids,
    tile_cols,
    adjacency,
    w_encode,
    w_fine,
    w_coarse,
    w_edge,
    w_sender,
    w_node_in,
    w_node_out,
    node_gain,
):
    rows, width = grid_feats.shape
    members = lax.axis_size("member")
    capacity = rows // 8
    nodes = mesh_states.shape[0]
    tile_side = adjacency.shape[2]
    tiles_dev = nodes // tile_side
    neighbours = coarse_ids.shape[1]
    messages = jax.nn.silu(
        jnp.dot(grid_feats, w_encode, preferred_element_type=jnp.float32)
    ).astype(jnp.bfloat16)
    owner = grid_owner[:, 0]
    slot = grid_slot[:, 0]
    onehot = (owner[:, None] == jnp.arange(members, dtype=jnp.int32)[None, :]).astype(jnp.int32)
    earlier_count = jnp.cumsum(onehot, axis=0) - onehot
    rank_row = jnp.sum(earlier_count * onehot, axis=1)
    dest = owner * capacity + rank_row
    send_rows = jnp.zeros((members * capacity, width), jnp.bfloat16).at[dest].set(messages)
    send_slots = jnp.full((members * capacity,), -1, jnp.int32).at[dest].set(slot)
    recv_rows, recv_slots = (
        lax.all_to_all(
            send_rows.reshape(members, capacity, width),
            "member",
            split_axis=0,
            concat_axis=0,
            tiled=True,
        ),
        lax.all_to_all(
            send_slots.reshape(members, capacity), "member", split_axis=0, concat_axis=0, tiled=True
        ),
    )
    target = jnp.where(recv_slots >= 0, recv_slots, nodes).reshape(-1)
    encoded = jax.ops.segment_sum(
        recv_rows.reshape(-1, width).astype(jnp.float32), target, num_segments=nodes + 1
    )[:nodes].astype(jnp.bfloat16)
    own_states = lax.all_gather(coarse_states, "member", axis=0, tiled=True)
    prior_states = from_behind(own_states, "group", 1)
    both_states = jnp.concatenate([own_states, prior_states], axis=0)
    table = jnp.dot(both_states, w_coarse, preferred_element_type=jnp.float32).astype(jnp.bfloat16)
    fine_part = jnp.dot(mesh_states, w_fine, preferred_element_type=jnp.float32)
    picked = table[coarse_ids]
    edge_hidden = jax.nn.silu(fine_part[:, None, :] + picked.astype(jnp.float32)).astype(
        jnp.bfloat16
    )
    edge_out = jnp.dot(
        edge_hidden.reshape(nodes * neighbours, width), w_edge, preferred_element_type=jnp.float32
    )
    coarse_sum = jnp.sum(edge_out.reshape(nodes, neighbours, width), axis=1).astype(jnp.bfloat16)
    sent = jax.nn.silu(jnp.dot(mesh_states, w_sender, preferred_element_type=jnp.float32)).astype(
        jnp.bfloat16
    )
    window = with_halo(sent, (("member", 0),), nodes)
    window_tiles = window.reshape(3 * tiles_dev, tile_side, width)
    chosen = window_tiles[tile_cols]
    mesh_sum = (
        jnp.einsum("rkij,rkjd->rid", adjacency, chosen, preferred_element_type=jnp.float32)
        .reshape(nodes, width)
        .astype(jnp.bfloat16)
    )
    joined = jnp.concatenate([mesh_states, encoded, coarse_sum, mesh_sum], axis=1)
    hidden = jax.nn.silu(jnp.dot(joined, w_node_in, preferred_element_type=jnp.float32)).astype(
        jnp.bfloat16
    )
    update = jnp.dot(hidden, w_node_out, preferred_element_type=jnp.float32)
    mean = jnp.mean(update, axis=1, keepdims=True)
    centred = update - mean
    variance = jnp.mean(centred * centred, axis=1, keepdims=True)
    normed = centred / jnp.sqrt(variance + 1e-05) * node_gain
    return (mesh_states.astype(jnp.float32) + normed).astype(jnp.bfloat16)


def body(groups, members, *args):
    grid_feats, grid_owner, grid_slot, mesh_states = args[:4]
    owner, slot = grid_owner[:, 0], grid_slot[:, 0]
    blk = mesh_states.shape[0] // members
    way = (slot // blk + owner) % members
    counts = jnp.sum((way[None, :] == jnp.arange(members)[:, None]).astype(jnp.int32), axis=1)
    most = lax.pmax(jnp.max(counts), ("group", "member"))
    quick = fast(groups, members, grid_feats, owner, slot, *args[3:])
    return lax.cond(most > PART, lambda: slow(*args), lambda: quick)


def solution(mesh):
    placed = (
        P(("group", "member"), None),
        P(("group", "member"), None),
        P(("group", "member"), None),
        P(("group", "member"), None),
        P(("group", "member"), None),
        P(("group", "member"), None),
        P(("group", "member"), None),
        P(("group", "member"), None, None, None),
        P(),
        P(),
        P(),
        P(),
        P(),
        P(),
        P(),
        P(),
    )
    groups, members = mesh.shape["group"], mesh.shape["member"]
    return jax.shard_map(
        functools.partial(body, groups, members), mesh=mesh, in_specs=placed, out_specs=P(("group", "member"), None), check_vma=False
    )
```

```python
import functools

import jax
import jax.numpy as jnp
from jax import lax
from jax.experimental import pallas as pl
from jax.experimental.pallas import tpu as pltpu
from jax.sharding import PartitionSpec as P

MESH = pl.DeviceIdType.MESH
F32 = jnp.float32
BF16 = jnp.bfloat16
LINE = 8
PART = 112
SLOT = 128


def silu(v):
    half = 0.5 * v
    return half + half * jnp.tanh(half)


def dot(a, b):
    return jnp.dot(a, b, preferred_element_type=F32)


def dot_t(a, b):
    return lax.dot_general(a, b, (((1,), (1,)), ((), ())), preferred_element_type=F32)


def kernel(
    groups,
    members,
    line,
    ids_ref,
    cols_ref,
    feats_ref,
    owner_ref,
    slot_ref,
    mesh_ref,
    coarse_ref,
    adj_ref,
    w_encode_ref,
    w_fine_ref,
    w_coarse_ref,
    w_edge_ref,
    w_sender_ref,
    w_in_ref,
    w_out_ref,
    gain_ref,
    out_ref,
    flag_ref,
    messages,
    send1,
    recv1,
    send_idx,
    recv_idx,
    table16,
    table32,
    window,
    picked,
    fine,
    partial,
    total,
    enc_send,
    enc,
    flag_send,
    flag_recv,
    s_a2a,
    r_a2a,
    s_idx,
    r_idx,
    s_enc,
    r_enc,
    s_line,
    r_line,
    s_plane,
    r_plane,
    s_next,
    r_next,
    s_halo,
    r_halo,
    s_flag,
    r_flag,
):
    me_g = lax.axis_index("group")
    me = lax.axis_index("member")
    lines = members // line
    my_line = me // line
    my_spot = me % line
    rows, width = feats_ref.shape
    nodes = mesh_ref.shape[0]
    own = coarse_ref.shape[0]
    neighbours = ids_ref.shape[0]
    lane = SLOT
    sides = width // lane
    tile = adj_ref.shape[2]
    tiles = adj_ref.shape[0]
    per_tile = adj_ref.shape[1]
    blk = nodes // members
    next_g = (me_g + 1) % groups

    def copy(src, dst, send, recv, group, member):
        return pltpu.make_async_remote_copy(
            src_ref=src,
            dst_ref=dst,
            send_sem=send,
            recv_sem=recv,
            device_id=(group, member),
            device_id_type=MESH,
        )

    barrier = pltpu.get_barrier_semaphore()

    @pl.loop(1, members)
    def _(d):
        pl.semaphore_signal(
            barrier, inc=1, device_id=(me_g, (me + d) % members), device_id_type=MESH
        )

    @pl.loop(1, groups)
    def _(d):
        pl.semaphore_signal(
            barrier, inc=1, device_id=((me_g + d) % groups, me), device_id_type=MESH
        )

    table16[0, my_line, pl.ds(pl.multiple_of(my_spot * own, own), own), :] = dot(
        coarse_ref[...], w_coarse_ref[...]
    ).astype(BF16)
    chunk = 256

    @pl.loop(0, nodes // chunk)
    def _(i):
        at = pl.ds(pl.multiple_of(i * chunk, chunk), chunk)
        per = chunk // tile
        part = silu(dot(mesh_ref[at, :], w_sender_ref[...])).astype(BF16)
        window[pl.ds(tiles + i * per, per)] = part.reshape(per, tile, width)

    @pl.when(me == 0)
    def _():
        window[0:tiles] = jnp.zeros((tiles, tile, width), BF16)

    @pl.when(me == members - 1)
    def _():
        window[2 * tiles : 3 * tiles] = jnp.zeros((tiles, tile, width), BF16)

    recv1[:, PART:, :] = jnp.zeros((members, SLOT - PART, width), BF16)

    pl.semaphore_wait(barrier, members + groups - 2)

    def line_copy(spot, way):
        at = pl.ds(pl.multiple_of((spot + line) % line * own, own), own)
        block = table16.at[0, my_line, at, :]
        to = my_line * line + (my_spot + way + line) % line
        sem = (spot + line) % line
        return copy(block, block, s_line.at[sem, (way + 1) // 2], r_line.at[sem], me_g, to)

    line_copy(my_spot, 1).start()
    line_copy(my_spot, -1).start()

    def line_step(d):
        line_copy(my_spot - d, 1).wait_recv()
        line_copy(my_spot - d, 1).start()
        if d < line // 2 - 1:
            line_copy(my_spot + d, -1).wait_recv()
            line_copy(my_spot + d, -1).start()

    def line_last():
        line_copy(my_spot - line // 2, 1).wait_recv()
        if line > 2:
            line_copy(my_spot + line // 2 - 1, -1).wait_recv()

    steps = list(range(1, line // 2))

    def halo_up():
        return copy(
            window.at[tiles : 2 * tiles],
            window.at[0:tiles],
            s_halo.at[0],
            r_halo.at[0],
            me_g,
            (me + 1) % members,
        )

    def halo_down():
        return copy(
            window.at[tiles : 2 * tiles],
            window.at[2 * tiles : 3 * tiles],
            s_halo.at[1],
            r_halo.at[1],
            me_g,
            (me + members - 1) % members,
        )

    @pl.when(me < members - 1)
    def _():
        halo_up().start()

    @pl.when(me > 0)
    def _():
        halo_down().start()

    parts = 4
    for part in range(parts):

        @pl.loop(0, rows // chunk // parts)
        def _(i):
            first = (part * (rows // chunk // parts) + i) * chunk
            at = pl.ds(pl.multiple_of(first, chunk), chunk)
            messages[at, :] = silu(dot(feats_ref[at, :], w_encode_ref[...])).astype(BF16)

        if part % 2 and part // 2 < len(steps) - 1:
            line_step(steps[part // 2])

    owner = owner_ref[...]
    slot = slot_ref[...]
    way = (slot // blk + owner) % members
    hot = (lax.broadcasted_iota(jnp.int32, (members, rows), 0) == way).astype(F32)
    hot16 = hot.astype(BF16)
    lanes = min(256, rows)
    upper = (
        lax.broadcasted_iota(jnp.int32, (lanes, lanes), 0)
        < lax.broadcasted_iota(jnp.int32, (lanes, lanes), 1)
    ).astype(BF16)
    before = jnp.zeros((members, 1), F32)
    ranks = []
    for b in range(rows // lanes):
        here = hot[:, b * lanes : (b + 1) * lanes]
        count = dot(hot16[:, b * lanes : (b + 1) * lanes], upper) + before
        ranks.append(jnp.sum(here * count, axis=0, keepdims=True))
        before = before + jnp.sum(here, axis=1, keepdims=True)
    rank = jnp.concatenate(ranks, axis=1).astype(jnp.int32)
    fits = rank < PART
    dest = jnp.where(fits, way * SLOT + rank, -1)
    stack = jnp.concatenate(
        [
            hot16,
            hot16 * owner.astype(F32).astype(BF16),
            hot16 * (slot % blk).astype(F32).astype(BF16),
        ],
        axis=0,
    )
    place = (
        lax.broadcasted_iota(jnp.int32, (SLOT, rows), 0) == jnp.where(fits, rank, -1)
    ).astype(BF16)
    found = dot_t(stack, place)
    index = jnp.where(
        found[:members] > 0.5,
        found[members : 2 * members] * blk + found[2 * members :],
        -1.0,
    ).astype(jnp.int32)
    over = jnp.max(before, axis=0, keepdims=True) > PART
    last = lax.broadcasted_iota(jnp.int32, (members, SLOT), 1) == SLOT - 1
    index = jnp.where(last & over, -2, index)
    for t in range(members):
        send_idx[t] = index[t : t + 1, :]

    cuts = 2
    cut = line * own // cuts

    def plane_copy(to_line, at_line, c):
        block = table16.at[0, at_line, c * cut : (c + 1) * cut, :]
        to = to_line * line + my_spot
        return copy(block, block, s_plane.at[to_line, c], r_plane.at[at_line, c], me_g, to)

    def next_copy(at_line, c):
        at = slice(c * cut, (c + 1) * cut)
        return copy(
            table16.at[0, at_line, at, :],
            table16.at[1, at_line, at, :],
            s_next.at[at_line, c],
            r_next.at[at_line, c],
            next_g,
            me,
        )

    def plane_start():
        line_last()
        for c in range(cuts):

            @pl.loop(1, lines)
            def _(d):
                plane_copy((my_line + d) % lines, my_line, c).start()

            next_copy(my_line, c).start()

    def row_copy(to, source):
        return copy(
            send1.at[to, 0:PART, :],
            recv1.at[source, 0:PART, :],
            s_a2a.at[to],
            r_a2a.at[source],
            me_g,
            to,
        )

    def idx_copy(to, source):
        return copy(
            send_idx.at[to], recv_idx.at[source], s_idx.at[to], r_idx.at[source], me_g, to
        )

    @pl.loop(1, members)
    def _(d):
        idx_copy((me + d) % members, me).start()

    if steps:
        line_step(steps[-1])

    batch = 4

    @pl.loop(0, members // batch)
    def _(step):
        @pl.when(step == min(2, members // batch - 1))
        def _():
            plane_start()

        first = ((me // batch + step) % (members // batch)) * batch
        spread = (
            lax.broadcasted_iota(jnp.int32, (batch * SLOT, rows), 0) + first * SLOT == dest
        ).astype(BF16)
        packed = dot(spread, messages[...]).astype(BF16)
        for j in range(batch):
            to = first + j
            send1[to] = packed[j * SLOT : (j + 1) * SLOT]

            @pl.when(to != me)
            def _():
                row_copy(to, me).start()

    recv1[me, 0:PART, :] = send1[me, 0:PART, :]
    recv_idx[me] = send_idx[me]

    @pl.loop(1, members)
    def _(d):
        idx_copy(me, (me + members - d) % members).wait_recv()

    flag_send[...] = jnp.where(jnp.min(recv_idx[...], axis=0) < -1, 1, 0)

    def flag_copy(to, source):
        return copy(flag_send, flag_recv.at[source], s_flag.at[to], r_flag.at[source], to, me)

    @pl.loop(1, groups)
    def _(d):
        flag_copy((me_g + d) % groups, me_g).start()

    flag_recv[me_g] = flag_send[...]

    @pl.loop(0, nodes // chunk)
    def _(i):
        at = pl.ds(pl.multiple_of(i * chunk, chunk), chunk)
        fine[at, :] = dot(mesh_ref[at, :], w_fine_ref[...])
        partial[at, :] = dot(mesh_ref[at, :], w_in_ref[0:width, :])

    @pl.when(me > 0)
    def _():
        halo_up().wait_recv()

    @pl.when(me < members - 1)
    def _():
        halo_down().wait_recv()

    @pl.loop(0, tiles)
    def _(r):
        acc = jnp.zeros((tile, width), F32)
        for j in range(per_tile):
            acc = acc + dot(adj_ref[r, j], window[cols_ref[j, r]])
        at = pl.ds(pl.multiple_of(r * tile, tile), tile)
        partial[at, :] += dot(acc.astype(BF16), w_in_ref[3 * width : 4 * width, :])

    for c in range(cuts):

        @pl.loop(1, lines)
        def _(d):
            at_line = (my_line + d) % lines
            plane_copy(my_line, at_line, c).wait_recv()
            next_copy(at_line, c).start()

    half = own * members

    def widen(part, at_line):
        at = pl.ds(pl.multiple_of(part * half + at_line * line * own, own), line * own)
        for h in range(sides):
            table32[h, at, :] = table16[part, at_line, :, h * lane : (h + 1) * lane].astype(F32)

    @pl.loop(0, lines)
    def _(i):
        widen(0, i)

    total[...] = jnp.zeros_like(total)

    @pl.loop(0, members // 2)
    def _(i):
        sources = [(me + members - 2 * i - j) % members for j in range(2)]
        for source in sources:

            @pl.when(source != me)
            def _():
                row_copy(me, source).wait_recv()

        index = jnp.concatenate([recv_idx[source] for source in sources], axis=1)
        block = jnp.concatenate([recv1[source] for source in sources], axis=0)
        spread = (
            lax.broadcasted_iota(jnp.int32, (nodes, 2 * SLOT), 0) == index
        ).astype(BF16)
        total[...] += dot(spread, block)

    enc_send[...] = total[...].astype(BF16)

    def enc_copy(to, source):
        there = (source + members - to) % members
        return copy(
            enc_send.at[pl.ds(pl.multiple_of(to * blk, blk), blk), :],
            enc.at[pl.ds(pl.multiple_of(there * blk, blk), blk), :],
            s_enc.at[to],
            r_enc.at[source],
            me_g,
            to,
        )

    @pl.loop(1, members)
    def _(d):
        enc_copy((me + d) % members, me).start()

    enc[0:blk, :] = enc_send[pl.ds(pl.multiple_of(me * blk, blk), blk), :]

    for c in range(cuts):

        @pl.loop(0, lines)
        def _(i):
            next_copy(i, c).wait_recv()

    @pl.loop(0, lines)
    def _(i):
        widen(1, i)

    unroll = 8

    @pl.loop(0, nodes // unroll)
    def _(i):
        for u in range(unroll):
            n = i * unroll + u
            for k in range(neighbours):
                at = pl.ds(ids_ref[k, n], 1)
                for h in range(sides):
                    picked[k, h, pl.ds(n, 1), :] = table32[h, at, :]

    @pl.loop(0, nodes // chunk)
    def _(i):
        at = pl.ds(pl.multiple_of(i * chunk, chunk), chunk)
        accs = []
        for h in range(sides):
            mine = fine[at, h * lane : (h + 1) * lane]
            acc = jnp.zeros((chunk, lane), F32)
            for k in range(neighbours):
                acc = acc + silu(mine + picked[k, h, at, :]).astype(BF16).astype(F32)
            accs.append(acc.astype(BF16))
        acc = jnp.concatenate(accs, axis=1)
        coarse_sum = dot(acc, w_edge_ref[...]).astype(BF16)
        partial[at, :] += dot(coarse_sum, w_in_ref[2 * width : 3 * width, :])

    @pl.loop(1, members)
    def _(d):
        enc_copy(me, (me + d) % members).wait_recv()

    @pl.loop(0, nodes // chunk)
    def _(i):
        at = pl.ds(pl.multiple_of(i * chunk, chunk), chunk)
        hidden = silu(partial[at, :] + dot(enc[at, :], w_in_ref[width : 2 * width, :]))
        update = dot(hidden.astype(BF16), w_out_ref[...])
        mean = jnp.mean(update, axis=1, keepdims=True)
        centred = update - mean
        variance = jnp.mean(centred * centred, axis=1, keepdims=True)
        normed = centred / jnp.sqrt(variance + 1e-05) * gain_ref[...]
        out_ref[at, :] = (mesh_ref[at, :].astype(F32) + normed).astype(BF16)

    @pl.loop(1, groups)
    def _(d):
        flag_copy(me_g, (me_g + d) % groups).wait_recv()

    flag_ref[...] = jnp.max(flag_recv[...], axis=0)

    @pl.loop(1, groups)
    def _(d):
        flag_copy((me_g + d) % groups, me_g).wait_send()

    for d in range(line // 2):
        line_copy(my_spot - d, 1).wait_send()
        if d < line // 2 - 1:
            line_copy(my_spot + d, -1).wait_send()

    for c in range(cuts):

        @pl.loop(1, lines)
        def _(d):
            plane_copy((my_line + d) % lines, my_line, c).wait_send()

        @pl.loop(0, lines)
        def _(i):
            next_copy(i, c).wait_send()

    @pl.when(me < members - 1)
    def _():
        halo_up().wait_send()

    @pl.when(me > 0)
    def _():
        halo_down().wait_send()

    @pl.loop(1, members)
    def _(d):
        to = (me + d) % members
        row_copy(to, me).wait_send()
        idx_copy(to, me).wait_send()
        enc_copy(to, me).wait_send()


def fast(
    groups,
    members,
    grid_feats,
    owner,
    slot,
    mesh_states,
    coarse_states,
    coarse_ids,
    tile_cols,
    adjacency,
    w_encode,
    w_fine,
    w_coarse,
    w_edge,
    w_sender,
    w_node_in,
    w_node_out,
    node_gain,
):
    rows, width = grid_feats.shape
    nodes = mesh_states.shape[0]
    own = coarse_states.shape[0]
    neighbours = coarse_ids.shape[1]
    tiles, per_tile, tile, _ = adjacency.shape
    line = min(LINE, members // 2)
    lines = members // line
    dma = pltpu.SemaphoreType.DMA
    vmem = pl.BlockSpec(memory_space=pltpu.VMEM)
    smem = pl.BlockSpec(memory_space=pltpu.SMEM)
    return pl.pallas_call(
        functools.partial(kernel, groups, members, line),
        out_shape=(
            jax.ShapeDtypeStruct((nodes, width), BF16),
            jax.ShapeDtypeStruct((1, SLOT), jnp.int32),
        ),
        in_specs=[smem] * 2 + [vmem] * 14,
        out_specs=(vmem, vmem),
        scratch_shapes=[
            pltpu.VMEM((rows, width), BF16),
            pltpu.VMEM((members, SLOT, width), BF16),
            pltpu.VMEM((members, SLOT, width), BF16),
            pltpu.VMEM((members, 1, SLOT), jnp.int32),
            pltpu.VMEM((members, 1, SLOT), jnp.int32),
            pltpu.VMEM((2, lines, line * own, width), BF16),
            pltpu.VMEM((width // SLOT, 2 * members * own, SLOT), F32),
            pltpu.VMEM((3 * tiles, tile, width), BF16),
            pltpu.VMEM((neighbours, width // SLOT, nodes, SLOT), F32),
            pltpu.VMEM((nodes, width), F32),
            pltpu.VMEM((nodes, width), F32),
            pltpu.VMEM((nodes, width), F32),
            pltpu.VMEM((nodes, width), BF16),
            pltpu.VMEM((nodes, width), BF16),
            pltpu.VMEM((1, SLOT), jnp.int32),
            pltpu.VMEM((groups, 1, SLOT), jnp.int32),
            dma((members,)),
            dma((members,)),
            dma((members,)),
            dma((members,)),
            dma((members,)),
            dma((members,)),
            dma((line, 2)),
            dma((line,)),
            dma((lines, 2)),
            dma((lines, 2)),
            dma((lines, 2)),
            dma((lines, 2)),
            dma((2,)),
            dma((2,)),
            dma((groups,)),
            dma((groups,)),
        ],
        compiler_params=pltpu.CompilerParams(
            collective_id=0, has_side_effects=True, vmem_limit_bytes=56 << 20
        ),
    )(
        coarse_ids.T,
        tile_cols.T,
        grid_feats,
        owner.reshape(1, rows),
        slot.reshape(1, rows),
        mesh_states,
        coarse_states,
        adjacency,
        w_encode,
        w_fine,
        w_coarse,
        w_edge,
        w_sender,
        w_node_in,
        w_node_out,
        node_gain.reshape(1, width),
    )


def from_behind(block, axis, distance):
    devices = range(lax.axis_size(axis))
    route = [((i - distance) % len(devices), i) for i in devices]
    return lax.ppermute(block, axis, route)


def with_halo(cells, sides, width):
    for axis, dim in sides:
        count = lax.axis_size(axis)
        ends = count - 1
        head = lax.slice_in_dim(cells, 0, width, axis=dim)
        tail = lax.slice_in_dim(cells, cells.shape[dim] - width, cells.shape[dim], axis=dim)
        cells = jnp.concatenate(
            [
                lax.ppermute(tail, axis, [(i, (i + 1) % count) for i in range(ends)]),
                cells,
                lax.ppermute(head, axis, [((i + 1) % count, i) for i in range(ends)]),
            ],
            axis=dim,
        )
    return cells


def slow(
    grid_feats,
    grid_owner,
    grid_slot,
    mesh_states,
    coarse_states,
    coarse_ids,
    tile_cols,
    adjacency,
    w_encode,
    w_fine,
    w_coarse,
    w_edge,
    w_sender,
    w_node_in,
    w_node_out,
    node_gain,
):
    rows, width = grid_feats.shape
    members = lax.axis_size("member")
    capacity = rows // 8
    nodes = mesh_states.shape[0]
    tile_side = adjacency.shape[2]
    tiles_dev = nodes // tile_side
    neighbours = coarse_ids.shape[1]
    messages = jax.nn.silu(
        jnp.dot(grid_feats, w_encode, preferred_element_type=jnp.float32)
    ).astype(jnp.bfloat16)
    owner = grid_owner[:, 0]
    slot = grid_slot[:, 0]
    onehot = (owner[:, None] == jnp.arange(members, dtype=jnp.int32)[None, :]).astype(jnp.int32)
    earlier_count = jnp.cumsum(onehot, axis=0) - onehot
    rank_row = jnp.sum(earlier_count * onehot, axis=1)
    dest = owner * capacity + rank_row
    send_rows = jnp.zeros((members * capacity, width), jnp.bfloat16).at[dest].set(messages)
    send_slots = jnp.full((members * capacity,), -1, jnp.int32).at[dest].set(slot)
    recv_rows, recv_slots = (
        lax.all_to_all(
            send_rows.reshape(members, capacity, width),
            "member",
            split_axis=0,
            concat_axis=0,
            tiled=True,
        ),
        lax.all_to_all(
            send_slots.reshape(members, capacity), "member", split_axis=0, concat_axis=0, tiled=True
        ),
    )
    target = jnp.where(recv_slots >= 0, recv_slots, nodes).reshape(-1)
    encoded = jax.ops.segment_sum(
        recv_rows.reshape(-1, width).astype(jnp.float32), target, num_segments=nodes + 1
    )[:nodes].astype(jnp.bfloat16)
    own_states = lax.all_gather(coarse_states, "member", axis=0, tiled=True)
    prior_states = from_behind(own_states, "group", 1)
    both_states = jnp.concatenate([own_states, prior_states], axis=0)
    table = jnp.dot(both_states, w_coarse, preferred_element_type=jnp.float32).astype(jnp.bfloat16)
    fine_part = jnp.dot(mesh_states, w_fine, preferred_element_type=jnp.float32)
    picked = table[coarse_ids]
    edge_hidden = jax.nn.silu(fine_part[:, None, :] + picked.astype(jnp.float32)).astype(
        jnp.bfloat16
    )
    edge_out = jnp.dot(
        edge_hidden.reshape(nodes * neighbours, width), w_edge, preferred_element_type=jnp.float32
    )
    coarse_sum = jnp.sum(edge_out.reshape(nodes, neighbours, width), axis=1).astype(jnp.bfloat16)
    sent = jax.nn.silu(jnp.dot(mesh_states, w_sender, preferred_element_type=jnp.float32)).astype(
        jnp.bfloat16
    )
    window = with_halo(sent, (("member", 0),), nodes)
    window_tiles = window.reshape(3 * tiles_dev, tile_side, width)
    chosen = window_tiles[tile_cols]
    mesh_sum = (
        jnp.einsum("rkij,rkjd->rid", adjacency, chosen, preferred_element_type=jnp.float32)
        .reshape(nodes, width)
        .astype(jnp.bfloat16)
    )
    joined = jnp.concatenate([mesh_states, encoded, coarse_sum, mesh_sum], axis=1)
    hidden = jax.nn.silu(jnp.dot(joined, w_node_in, preferred_element_type=jnp.float32)).astype(
        jnp.bfloat16
    )
    update = jnp.dot(hidden, w_node_out, preferred_element_type=jnp.float32)
    mean = jnp.mean(update, axis=1, keepdims=True)
    centred = update - mean
    variance = jnp.mean(centred * centred, axis=1, keepdims=True)
    normed = centred / jnp.sqrt(variance + 1e-05) * node_gain
    return (mesh_states.astype(jnp.float32) + normed).astype(jnp.bfloat16)


def body(groups, members, *args):
    grid_feats, grid_owner, grid_slot = args[:3]
    quick, left_out = fast(groups, members, grid_feats, grid_owner, grid_slot, *args[3:])
    return lax.cond(left_out[0, SLOT - 1] > 0, lambda: slow(*args), lambda: quick)


def solution(mesh):
    placed = (
        P(("group", "member"), None),
        P(("group", "member"), None),
        P(("group", "member"), None),
        P(("group", "member"), None),
        P(("group", "member"), None),
        P(("group", "member"), None),
        P(("group", "member"), None),
        P(("group", "member"), None, None, None),
        P(),
        P(),
        P(),
        P(),
        P(),
        P(),
        P(),
        P(),
    )
    groups, members = mesh.shape["group"], mesh.shape["member"]
    return jax.shard_map(
        functools.partial(body, groups, members), mesh=mesh, in_specs=placed, out_specs=P(("group", "member"), None), check_vma=False
    )
```

```python
import functools

import jax
import jax.numpy as jnp
from jax import lax
from jax.experimental import pallas as pl
from jax.experimental.pallas import tpu as pltpu
from jax.sharding import PartitionSpec as P

MESH = pl.DeviceIdType.MESH
F32 = jnp.float32
BF16 = jnp.bfloat16
LINE = 8
PART = 96
LANES = 128
PLANS = 4


def silu(v):
    half = 0.5 * v
    return half + half * jnp.tanh(half)


def dot(a, b):
    return jnp.dot(a, b, preferred_element_type=F32)


def dot_t(a, b):
    return lax.dot_general(a, b, (((1,), (1,)), ((), ())), preferred_element_type=F32)


def kernel(
    groups,
    members,
    line,
    ids_ref,
    cols_ref,
    feats_ref,
    owner_ref,
    slot_ref,
    mesh_ref,
    coarse_ref,
    adj_ref,
    w_encode_ref,
    w_fine_ref,
    w_coarse_ref,
    w_edge_ref,
    w_sender_ref,
    w_in_ref,
    w_out_ref,
    gain_ref,
    out_ref,
    flag_ref,
    messages,
    send1,
    recv1,
    send_idx,
    recv_idx,
    table16,
    table32,
    window,
    picked,
    fine,
    partial,
    total,
    enc_send,
    enc,
    flag_send,
    flag_recv,
    s_a2a,
    r_a2a,
    s_idx,
    r_idx,
    s_enc,
    r_enc,
    s_line,
    r_line,
    s_plane,
    r_plane,
    s_next,
    r_next,
    s_halo,
    r_halo,
    s_flag,
    r_flag,
    send_score,
    recv_score,
    s_score,
    r_score,
):
    me_g = lax.axis_index("group")
    me = lax.axis_index("member")
    lines = members // line
    my_line = me // line
    my_spot = me % line
    rows, width = feats_ref.shape
    nodes = mesh_ref.shape[0]
    own = coarse_ref.shape[0]
    neighbours = ids_ref.shape[0]
    lane = LANES
    sides = width // lane
    tile = adj_ref.shape[2]
    tiles = adj_ref.shape[0]
    per_tile = adj_ref.shape[1]
    blk = nodes // members
    next_g = (me_g + 1) % groups

    def copy(src, dst, send, recv, group, member):
        return pltpu.make_async_remote_copy(
            src_ref=src,
            dst_ref=dst,
            send_sem=send,
            recv_sem=recv,
            device_id=(group, member),
            device_id_type=MESH,
        )

    plans = min(PLANS, members)
    turn = members // plans
    owner = owner_ref[...]
    slot = slot_ref[...]
    spots = lax.broadcasted_iota(jnp.int32, (members, rows), 0)

    def way_of(plan):
        return (slot // blk + owner * (1 + turn * plan)) % members

    barrier = pltpu.get_barrier_semaphore()

    @pl.loop(1, members)
    def _(d):
        pl.semaphore_signal(
            barrier, inc=1, device_id=(me_g, (me + d) % members), device_id_type=MESH
        )

    @pl.loop(1, groups)
    def _(d):
        pl.semaphore_signal(
            barrier, inc=1, device_id=((me_g + d) % groups, me), device_id_type=MESH
        )

    table16[0, my_line, pl.ds(pl.multiple_of(my_spot * own, own), own), :] = dot(
        coarse_ref[...], w_coarse_ref[...]
    ).astype(BF16)
    chunk = 256

    @pl.loop(0, nodes // chunk)
    def _(i):
        at = pl.ds(pl.multiple_of(i * chunk, chunk), chunk)
        per = chunk // tile
        part = silu(dot(mesh_ref[at, :], w_sender_ref[...])).astype(BF16)
        window[pl.ds(tiles + i * per, per)] = part.reshape(per, tile, width)

    @pl.when(me == 0)
    def _():
        window[0:tiles] = jnp.zeros((tiles, tile, width), BF16)

    @pl.when(me == members - 1)
    def _():
        window[2 * tiles : 3 * tiles] = jnp.zeros((tiles, tile, width), BF16)

    lanes_of = lax.broadcasted_iota(jnp.int32, (1, LANES), 1)
    score = jnp.zeros((1, LANES), jnp.int32)
    for plan in range(plans):
        counts = jnp.sum((spots == way_of(plan)).astype(F32), axis=1, keepdims=True)
        most = jnp.max(counts, axis=0, keepdims=True).astype(jnp.int32)
        score = jnp.where(lanes_of == plan, most, score)
    send_score[...] = score
    recv_score[me] = score

    pl.semaphore_wait(barrier, members + groups - 2)

    def score_copy(to, source):
        return copy(
            send_score, recv_score.at[source], s_score.at[to], r_score.at[source], me_g, to
        )

    @pl.loop(1, members)
    def _(d):
        score_copy((me + d) % members, me).start()

    def line_copy(spot, way):
        at = pl.ds(pl.multiple_of((spot + line) % line * own, own), own)
        block = table16.at[0, my_line, at, :]
        to = my_line * line + (my_spot + way + line) % line
        sem = (spot + line) % line
        return copy(block, block, s_line.at[sem, (way + 1) // 2], r_line.at[sem], me_g, to)

    line_copy(my_spot, 1).start()
    line_copy(my_spot, -1).start()

    def line_step(d):
        line_copy(my_spot - d, 1).wait_recv()
        line_copy(my_spot - d, 1).start()
        if d < line // 2 - 1:
            line_copy(my_spot + d, -1).wait_recv()
            line_copy(my_spot + d, -1).start()

    def line_last():
        line_copy(my_spot - line // 2, 1).wait_recv()
        if line > 2:
            line_copy(my_spot + line // 2 - 1, -1).wait_recv()

    steps = list(range(1, line // 2))

    def halo_up():
        return copy(
            window.at[tiles : 2 * tiles],
            window.at[0:tiles],
            s_halo.at[0],
            r_halo.at[0],
            me_g,
            (me + 1) % members,
        )

    def halo_down():
        return copy(
            window.at[tiles : 2 * tiles],
            window.at[2 * tiles : 3 * tiles],
            s_halo.at[1],
            r_halo.at[1],
            me_g,
            (me + members - 1) % members,
        )

    def halo_start():
        @pl.when(me < members - 1)
        def _():
            halo_up().start()

        @pl.when(me > 0)
        def _():
            halo_down().start()

    halo_start()

    @pl.loop(0, rows // chunk)
    def _(i):
        at = pl.ds(pl.multiple_of(i * chunk, chunk), chunk)
        messages[at, :] = silu(dot(feats_ref[at, :], w_encode_ref[...])).astype(BF16)

    @pl.loop(1, members)
    def _(d):
        score_copy(me, (me + d) % members).wait_recv()

    worst = jnp.max(recv_score[...], axis=0)
    plan = jnp.zeros((1, 1), jnp.int32)
    for p in range(plans - 1, 0, -1):
        rest = jnp.where(worst[:, p : p + 1] <= PART, p, plan)
        plan = rest
    plan = jnp.where(worst[:, 0:1] <= PART, 0, plan)
    way = way_of(plan)
    hot = (spots == way).astype(F32)
    hot16 = hot.astype(BF16)
    lanes = min(256, rows)
    upper = (
        lax.broadcasted_iota(jnp.int32, (lanes, lanes), 0)
        < lax.broadcasted_iota(jnp.int32, (lanes, lanes), 1)
    ).astype(BF16)
    before = jnp.zeros((members, 1), F32)
    ranks = []
    for b in range(rows // lanes):
        here = hot[:, b * lanes : (b + 1) * lanes]
        count = dot(hot16[:, b * lanes : (b + 1) * lanes], upper) + before
        ranks.append(jnp.sum(here * count, axis=0, keepdims=True))
        before = before + jnp.sum(here, axis=1, keepdims=True)
    rank = jnp.concatenate(ranks, axis=1).astype(jnp.int32)
    fits = rank < PART
    dest = jnp.where(fits, way * PART + rank, -1)
    stack = jnp.concatenate(
        [
            hot16,
            hot16 * owner.astype(F32).astype(BF16),
            hot16 * (slot % blk).astype(F32).astype(BF16),
        ],
        axis=0,
    )
    place = (
        lax.broadcasted_iota(jnp.int32, (LANES, rows), 0) == jnp.where(fits, rank, -1)
    ).astype(BF16)
    found = dot_t(stack, place)
    index = jnp.where(
        found[:members] > 0.5,
        found[members : 2 * members] * blk + found[2 * members :],
        -1.0,
    ).astype(jnp.int32)
    over = jnp.max(before, axis=0, keepdims=True) > PART
    last = lax.broadcasted_iota(jnp.int32, (members, LANES), 1) == LANES - 1
    index = jnp.where(last & over, -2, index)
    for t in range(members):
        send_idx[t] = index[t : t + 1, :]

    cuts = 2
    cut = line * own // cuts
    after, ahead = (my_line + 1) % lines, (my_line + lines - 1) % lines

    def plane_copy(at_line, way, c):
        block = table16.at[0, at_line, c * cut : (c + 1) * cut, :]
        to = (my_line + way + lines) % lines * line + my_spot
        sem = s_plane.at[at_line, (way + 1) // 2, c]
        return copy(block, block, sem, r_plane.at[at_line, c], me_g, to)

    def next_copy(at_line, c):
        at = slice(c * cut, (c + 1) * cut)
        return copy(
            table16.at[0, at_line, at, :],
            table16.at[1, at_line, at, :],
            s_next.at[at_line, c],
            r_next.at[at_line, c],
            next_g,
            me,
        )

    ways = [1] if lines == 2 else [1, -1]

    def plane_start():
        line_last()
        for c in range(cuts):
            for way in ways:
                plane_copy(my_line, way, c).start()
            next_copy(my_line, c).start()

    def plane_middle():
        if lines > 2:
            plane_copy(ahead, 1, 0).wait_recv()
            plane_copy(ahead, 1, 0).start()
            next_copy(ahead, 0).start()
            plane_copy(after, -1, 1).wait_recv()
            plane_copy(after, -1, 1).start()
            next_copy(after, 1).start()
            plane_copy(ahead, 1, 1).wait_recv()
            next_copy(ahead, 1).start()
            plane_copy(after, -1, 0).wait_recv()
            next_copy(after, 0).start()

    def plane_last():
        across = (my_line + lines // 2) % lines
        for c in range(cuts):
            plane_copy(across, 1, c).wait_recv()
            next_copy(across, c).start()

    def plane_done():
        for c in range(cuts):
            for way in ways:
                plane_copy(my_line, way, c).wait_send()
        if lines > 2:
            plane_copy(ahead, 1, 0).wait_send()
            plane_copy(after, -1, 1).wait_send()

    def row_copy(to, source):
        return copy(
            send1.at[to],
            recv1.at[source],
            s_a2a.at[to],
            r_a2a.at[source],
            me_g,
            to,
        )

    def idx_copy(to, source):
        return copy(
            send_idx.at[to], recv_idx.at[source], s_idx.at[to], r_idx.at[source], me_g, to
        )

    @pl.loop(1, members)
    def _(d):
        idx_copy((me + d) % members, me).start()

    batch = 4

    @pl.loop(0, members // batch)
    def _(step):
        for i, d in enumerate(steps[:-1]):

            @pl.when(step == 2 + 4 * i)
            def _():
                line_step(d)

        spread = (
            lax.broadcasted_iota(jnp.int32, (batch * PART, rows), 0) + step * (batch * PART)
            == dest
        ).astype(BF16)
        packed = dot(spread, messages[...]).astype(BF16)
        send1[pl.ds(step * batch, batch)] = packed.reshape(batch, PART, width)

    if steps:
        line_step(steps[-1])

    @pl.loop(1, members)
    def _(d):
        row_copy((me + d) % members, me).start()

    plane_start()

    recv1[me] = send1[me]
    recv_idx[me] = send_idx[me]

    @pl.loop(0, nodes // chunk)
    def _(i):
        at = pl.ds(pl.multiple_of(i * chunk, chunk), chunk)
        fine[at, :] = dot(mesh_ref[at, :], w_fine_ref[...])
        partial[at, :] = dot(mesh_ref[at, :], w_in_ref[0:width, :])


    @pl.loop(1, members)
    def _(d):
        idx_copy(me, (me + members - d) % members).wait_recv()

    flag_send[...] = jnp.where(jnp.min(recv_idx[...], axis=0) < -1, 1, 0)

    def flag_copy(to, source):
        return copy(flag_send, flag_recv.at[source], s_flag.at[to], r_flag.at[source], to, me)

    @pl.loop(1, groups)
    def _(d):
        flag_copy((me_g + d) % groups, me_g).start()

    flag_recv[me_g] = flag_send[...]

    @pl.when(me > 0)
    def _():
        halo_up().wait_recv()

    @pl.when(me < members - 1)
    def _():
        halo_down().wait_recv()

    @pl.loop(0, tiles)
    def _(r):
        acc = jnp.zeros((tile, width), F32)
        for j in range(per_tile):
            acc = acc + dot(adj_ref[r, j], window[cols_ref[j, r]])
        at = pl.ds(pl.multiple_of(r * tile, tile), tile)
        partial[at, :] += dot(acc.astype(BF16), w_in_ref[3 * width : 4 * width, :])

    half = own * members

    def widen(part, at_line):
        at = pl.ds(pl.multiple_of(part * half + at_line * line * own, own), line * own)
        for h in range(sides):
            table32[h, at, :] = table16[part, at_line, :, h * lane : (h + 1) * lane].astype(F32)

    def enc_copy(to, source):
        there = (source + members - to) % members
        return copy(
            enc_send.at[pl.ds(pl.multiple_of(to * blk, blk), blk), :],
            enc.at[pl.ds(pl.multiple_of(there * blk, blk), blk), :],
            s_enc.at[to],
            r_enc.at[source],
            me_g,
            to,
        )

    plane_middle()
    plane_last()

    @pl.loop(0, lines)
    def _(i):
        widen(0, i)

    total[...] = jnp.zeros_like(total)

    together = min(8, members)

    @pl.loop(0, members // together)
    def _(i):
        sources = [(me + members - together * i - j) % members for j in range(together)]
        for source in sources:

            @pl.when(source != me)
            def _():
                row_copy(me, source).wait_recv()

        index = jnp.concatenate([recv_idx[source][:, :PART] for source in sources], axis=1)
        block = jnp.concatenate([recv1[source] for source in sources], axis=0)
        spread = (
            lax.broadcasted_iota(jnp.int32, (nodes, together * PART), 0) == index
        ).astype(BF16)
        total[...] += dot(spread, block)

    enc_send[...] = total[...].astype(BF16)

    @pl.loop(1, members)
    def _(d):
        enc_copy((me + d) % members, me).start()

    enc[0:blk, :] = enc_send[pl.ds(pl.multiple_of(me * blk, blk), blk), :]

    for c in range(cuts):

        @pl.loop(0, lines)
        def _(i):
            next_copy(i, c).wait_recv()

    @pl.loop(0, lines)
    def _(i):
        widen(1, i)

    unroll = 8

    @pl.loop(0, nodes // unroll)
    def _(i):
        for u in range(unroll):
            n = i * unroll + u
            for k in range(neighbours):
                at = pl.ds(ids_ref[k, n], 1)
                for h in range(sides):
                    picked[k, h, pl.ds(n, 1), :] = table32[h, at, :]

    @pl.loop(0, nodes // chunk)
    def _(i):
        at = pl.ds(pl.multiple_of(i * chunk, chunk), chunk)
        accs = []
        for h in range(sides):
            mine = fine[at, h * lane : (h + 1) * lane]
            acc = jnp.zeros((chunk, lane), F32)
            for k in range(neighbours):
                acc = acc + silu(mine + picked[k, h, at, :]).astype(BF16).astype(F32)
            accs.append(acc.astype(BF16))
        acc = jnp.concatenate(accs, axis=1)
        coarse_sum = dot(acc, w_edge_ref[...]).astype(BF16)
        partial[at, :] += dot(coarse_sum, w_in_ref[2 * width : 3 * width, :])

    @pl.loop(1, members)
    def _(d):
        enc_copy(me, (me + d) % members).wait_recv()

    assert nodes // chunk == plans

    @pl.loop(0, nodes // chunk)
    def _(i):
        at = pl.ds(pl.multiple_of(i * chunk, chunk), chunk)
        arrived = enc[at, :]
        for p in range(1, plans):
            there = pl.ds(pl.multiple_of((i + p * me) % plans * chunk, chunk), chunk)
            arrived = jnp.where(plan == p, enc[there, :], arrived)
        hidden = silu(
            partial[at, :]
            + dot(arrived, w_in_ref[width : 2 * width, :])
        )
        update = dot(hidden.astype(BF16), w_out_ref[...])
        mean = jnp.mean(update, axis=1, keepdims=True)
        centred = update - mean
        variance = jnp.mean(centred * centred, axis=1, keepdims=True)
        normed = centred / jnp.sqrt(variance + 1e-05) * gain_ref[...]
        out_ref[at, :] = (mesh_ref[at, :].astype(F32) + normed).astype(BF16)

    @pl.loop(1, groups)
    def _(d):
        flag_copy(me_g, (me_g + d) % groups).wait_recv()

    flag_ref[...] = jnp.max(flag_recv[...], axis=0)

    @pl.loop(1, members)
    def _(d):
        score_copy((me + d) % members, me).wait_send()

    @pl.loop(1, groups)
    def _(d):
        flag_copy((me_g + d) % groups, me_g).wait_send()

    for d in range(line // 2):
        line_copy(my_spot - d, 1).wait_send()
        if d < line // 2 - 1:
            line_copy(my_spot + d, -1).wait_send()

    plane_done()
    for c in range(cuts):

        @pl.loop(0, lines)
        def _(i):
            next_copy(i, c).wait_send()

    @pl.when(me < members - 1)
    def _():
        halo_up().wait_send()

    @pl.when(me > 0)
    def _():
        halo_down().wait_send()

    @pl.loop(1, members)
    def _(d):
        to = (me + d) % members
        idx_copy(to, me).wait_send()
        row_copy(to, me).wait_send()
        enc_copy(to, me).wait_send()


def fast(
    groups,
    members,
    grid_feats,
    owner,
    slot,
    mesh_states,
    coarse_states,
    coarse_ids,
    tile_cols,
    adjacency,
    w_encode,
    w_fine,
    w_coarse,
    w_edge,
    w_sender,
    w_node_in,
    w_node_out,
    node_gain,
):
    rows, width = grid_feats.shape
    nodes = mesh_states.shape[0]
    own = coarse_states.shape[0]
    neighbours = coarse_ids.shape[1]
    tiles, per_tile, tile, _ = adjacency.shape
    line = min(LINE, members // 2)
    lines = members // line
    dma = pltpu.SemaphoreType.DMA
    vmem = pl.BlockSpec(memory_space=pltpu.VMEM)
    smem = pl.BlockSpec(memory_space=pltpu.SMEM)
    return pl.pallas_call(
        functools.partial(kernel, groups, members, line),
        out_shape=(
            jax.ShapeDtypeStruct((nodes, width), BF16),
            jax.ShapeDtypeStruct((1, LANES), jnp.int32),
        ),
        in_specs=[smem] * 2 + [vmem] * 14,
        out_specs=(vmem, vmem),
        scratch_shapes=[
            pltpu.VMEM((rows, width), BF16),
            pltpu.VMEM((members, PART, width), BF16),
            pltpu.VMEM((members, PART, width), BF16),
            pltpu.VMEM((members, 1, LANES), jnp.int32),
            pltpu.VMEM((members, 1, LANES), jnp.int32),
            pltpu.VMEM((2, lines, line * own, width), BF16),
            pltpu.VMEM((width // LANES, 2 * members * own, LANES), F32),
            pltpu.VMEM((3 * tiles, tile, width), BF16),
            pltpu.VMEM((neighbours, width // LANES, nodes, LANES), F32),
            pltpu.VMEM((nodes, width), F32),
            pltpu.VMEM((nodes, width), F32),
            pltpu.VMEM((nodes, width), F32),
            pltpu.VMEM((nodes, width), BF16),
            pltpu.VMEM((nodes, width), BF16),
            pltpu.VMEM((1, LANES), jnp.int32),
            pltpu.VMEM((groups, 1, LANES), jnp.int32),
            dma((members,)),
            dma((members,)),
            dma((members,)),
            dma((members,)),
            dma((members,)),
            dma((members,)),
            dma((line, 2)),
            dma((line,)),
            dma((lines, 2, 2)),
            dma((lines, 2)),
            dma((lines, 2)),
            dma((lines, 2)),
            dma((2,)),
            dma((2,)),
            dma((groups,)),
            dma((groups,)),
            pltpu.VMEM((1, LANES), jnp.int32),
            pltpu.VMEM((members, 1, LANES), jnp.int32),
            dma((members,)),
            dma((members,)),
        ],
        compiler_params=pltpu.CompilerParams(
            collective_id=0, has_side_effects=True, vmem_limit_bytes=56 << 20
        ),
    )(
        coarse_ids.T,
        tile_cols.T,
        grid_feats,
        owner.reshape(1, rows),
        slot.reshape(1, rows),
        mesh_states,
        coarse_states,
        adjacency,
        w_encode,
        w_fine,
        w_coarse,
        w_edge,
        w_sender,
        w_node_in,
        w_node_out,
        node_gain.reshape(1, width),
    )


def from_behind(block, axis, distance):
    devices = range(lax.axis_size(axis))
    route = [((i - distance) % len(devices), i) for i in devices]
    return lax.ppermute(block, axis, route)


def with_halo(cells, sides, width):
    for axis, dim in sides:
        count = lax.axis_size(axis)
        ends = count - 1
        head = lax.slice_in_dim(cells, 0, width, axis=dim)
        tail = lax.slice_in_dim(cells, cells.shape[dim] - width, cells.shape[dim], axis=dim)
        cells = jnp.concatenate(
            [
                lax.ppermute(tail, axis, [(i, (i + 1) % count) for i in range(ends)]),
                cells,
                lax.ppermute(head, axis, [((i + 1) % count, i) for i in range(ends)]),
            ],
            axis=dim,
        )
    return cells


def slow(
    grid_feats,
    grid_owner,
    grid_slot,
    mesh_states,
    coarse_states,
    coarse_ids,
    tile_cols,
    adjacency,
    w_encode,
    w_fine,
    w_coarse,
    w_edge,
    w_sender,
    w_node_in,
    w_node_out,
    node_gain,
):
    rows, width = grid_feats.shape
    members = lax.axis_size("member")
    capacity = rows // 8
    nodes = mesh_states.shape[0]
    tile_side = adjacency.shape[2]
    tiles_dev = nodes // tile_side
    neighbours = coarse_ids.shape[1]
    messages = jax.nn.silu(
        jnp.dot(grid_feats, w_encode, preferred_element_type=jnp.float32)
    ).astype(jnp.bfloat16)
    owner = grid_owner[:, 0]
    slot = grid_slot[:, 0]
    onehot = (owner[:, None] == jnp.arange(members, dtype=jnp.int32)[None, :]).astype(jnp.int32)
    earlier_count = jnp.cumsum(onehot, axis=0) - onehot
    rank_row = jnp.sum(earlier_count * onehot, axis=1)
    dest = owner * capacity + rank_row
    send_rows = jnp.zeros((members * capacity, width), jnp.bfloat16).at[dest].set(messages)
    send_slots = jnp.full((members * capacity,), -1, jnp.int32).at[dest].set(slot)
    recv_rows, recv_slots = (
        lax.all_to_all(
            send_rows.reshape(members, capacity, width),
            "member",
            split_axis=0,
            concat_axis=0,
            tiled=True,
        ),
        lax.all_to_all(
            send_slots.reshape(members, capacity), "member", split_axis=0, concat_axis=0, tiled=True
        ),
    )
    target = jnp.where(recv_slots >= 0, recv_slots, nodes).reshape(-1)
    encoded = jax.ops.segment_sum(
        recv_rows.reshape(-1, width).astype(jnp.float32), target, num_segments=nodes + 1
    )[:nodes].astype(jnp.bfloat16)
    own_states = lax.all_gather(coarse_states, "member", axis=0, tiled=True)
    prior_states = from_behind(own_states, "group", 1)
    both_states = jnp.concatenate([own_states, prior_states], axis=0)
    table = jnp.dot(both_states, w_coarse, preferred_element_type=jnp.float32).astype(jnp.bfloat16)
    fine_part = jnp.dot(mesh_states, w_fine, preferred_element_type=jnp.float32)
    picked = table[coarse_ids]
    edge_hidden = jax.nn.silu(fine_part[:, None, :] + picked.astype(jnp.float32)).astype(
        jnp.bfloat16
    )
    edge_out = jnp.dot(
        edge_hidden.reshape(nodes * neighbours, width), w_edge, preferred_element_type=jnp.float32
    )
    coarse_sum = jnp.sum(edge_out.reshape(nodes, neighbours, width), axis=1).astype(jnp.bfloat16)
    sent = jax.nn.silu(jnp.dot(mesh_states, w_sender, preferred_element_type=jnp.float32)).astype(
        jnp.bfloat16
    )
    window = with_halo(sent, (("member", 0),), nodes)
    window_tiles = window.reshape(3 * tiles_dev, tile_side, width)
    chosen = window_tiles[tile_cols]
    mesh_sum = (
        jnp.einsum("rkij,rkjd->rid", adjacency, chosen, preferred_element_type=jnp.float32)
        .reshape(nodes, width)
        .astype(jnp.bfloat16)
    )
    joined = jnp.concatenate([mesh_states, encoded, coarse_sum, mesh_sum], axis=1)
    hidden = jax.nn.silu(jnp.dot(joined, w_node_in, preferred_element_type=jnp.float32)).astype(
        jnp.bfloat16
    )
    update = jnp.dot(hidden, w_node_out, preferred_element_type=jnp.float32)
    mean = jnp.mean(update, axis=1, keepdims=True)
    centred = update - mean
    variance = jnp.mean(centred * centred, axis=1, keepdims=True)
    normed = centred / jnp.sqrt(variance + 1e-05) * node_gain
    return (mesh_states.astype(jnp.float32) + normed).astype(jnp.bfloat16)


def body(groups, members, *args):
    grid_feats, grid_owner, grid_slot = args[:3]
    quick, left_out = fast(groups, members, grid_feats, grid_owner, grid_slot, *args[3:])
    return lax.cond(left_out[0, LANES - 1] > 0, lambda: slow(*args), lambda: quick)


def solution(mesh):
    placed = (
        P(("group", "member"), None),
        P(("group", "member"), None),
        P(("group", "member"), None),
        P(("group", "member"), None),
        P(("group", "member"), None),
        P(("group", "member"), None),
        P(("group", "member"), None),
        P(("group", "member"), None, None, None),
        P(),
        P(),
        P(),
        P(),
        P(),
        P(),
        P(),
        P(),
    )
    groups, members = mesh.shape["group"], mesh.shape["member"]
    return jax.shard_map(
        functools.partial(body, groups, members), mesh=mesh, in_specs=placed, out_specs=P(("group", "member"), None), check_vma=False
    )
```
